32 devices in a mesh: groups: 2 (over y), expert: 16 (over z, x, core), tensor: 1.
Axes of the slice: x: 2, y: 2, z: 4, core: 2. Of those that a mesh axis runs over, the one named last changes fastest.
Arguments:
- tokens: bfloat16 [512, 2048], P(('groups', 'expert')), parts along dimension 0, may hold values from -6 to 6
- expert_ids: int32 [512, 8], P(('groups', 'expert')), parts along dimension 0, may hold values from 0 to 15, all different within a row; in each aligned block of 16 rows (0 to 15, 16 to 31, ...) at most 16 rows name the same one
- keep_flags: int32 [512, 8], P(('groups', 'expert')), parts along dimension 0, may hold values 0 or 1
- router_weights: float32 [512, 8], P(('groups', 'expert')), parts along dimension 0, may hold values from 0.05 to 1
- grad_out: bfloat16 [512, 2048], P(('groups', 'expert'), 'tensor'), parts along dimension 0, may hold values from -6 to 6
- gate_weight: bfloat16 [16, 2048, 768], P('expert', None, 'tensor'), may hold values from -0.125 to 0.125
- up_weight: bfloat16 [16, 2048, 768], P('expert', None, 'tensor'), may hold values from -0.125 to 0.125
- down_weight: bfloat16 [16, 768, 2048], P('expert', 'tensor'), may hold values from -0.21875 to 0.21875
Outputs:
- combined: bfloat16 [512, 2048], P(('groups', 'expert'), 'tensor'), parts along dimension 0
- grad_tokens: bfloat16 [512, 2048], P(('groups', 'expert'), 'tensor'), parts along dimension 0
- grad_weights: float32 [512, 8], P(('groups', 'expert')), parts along dimension 0
The draws below stay inside these ranges and needn't reach their ends.
There are 2 independent parts, one for each index of `groups`. The reference program is written for one: setup_inputs(seed, part) draws one part's arguments, and reference() takes and returns one part's arrays. A program takes and returns all parts, laid end to end along the dimension named above; an argument that names none is the same for every part. Nothing has to cross between parts.
Inputs may be any that keep to these rules, and one draw needn't show every extreme that they name: `expert_ids`: each row names 8 different experts and every expert is named by some row. Among the 16 rows of one device (aligned blocks) no expert is named more than 16 times, a bound that some block reaches.
All inputs are finite; a program needn't handle non-finite values. No bound on the sum of `keep_flags` on one device may be relied on, other than what follows from the above.
Results may differ from the reference program's by a relative error of at most 0.0071.
Values may be sent and summed in bfloat16 or wider, within the bound.
A program may use at most 64 MiB of HBM per device.

```python
import math
import jax
import jax.numpy as jnp
import numpy as np
from jax import lax

D = 2048
HID = 768
TOPK = 8
TOK_DEV = 16
EXPERTS = 16
CAP = 16
HID_BLOCKS = 1
TOKENS = 256
N_EXPERT = 16


def touch_ends(entries, key, low, high):
    dims = entries.shape
    spot = [jax.random.randint(jax.random.fold_in(key, axis), (), 0, dims[axis]) for axis in range(len(dims))]
    entries = entries.at[tuple(spot)].set(low)
    longest = dims.index(max(dims))
    spot[longest] = (spot[longest] + 1) % dims[longest]
    return entries.at[tuple(spot)].set(high)


def shard_levels(stream_key, shape, cuts, smallest, top_value):
    factor_of, own = 1.0, jax.random.fold_in(stream_key, 6)
    for dim, parts in cuts:
        draws = jnp.exp(jax.random.uniform(jax.random.fold_in(own, dim), (parts,), jnp.float32, smallest / len(cuts), top_value / len(cuts)))
        factor_of = factor_of * jnp.repeat(draws, shape[dim] // parts).reshape([-1 if axis == dim else 1 for axis in range(len(shape))])
    return factor_of


def deal_out(stream_key, own, number, rows, number_of, top, limit, slope):
    order = jax.random.permutation(stream_key, number_of)
    crowded, usual = load_shares(number_of, rows * top, limit, slope, True), load_shares(number_of, rows * top, limit, slope, False)
    places = jnp.arange(number_of)

    def named(sizes, offset_by):
        used = int((sizes > 0).sum())
        fixed = max(1, used // 4)
        passed = fixed + (places - fixed + offset_by * (used - fixed)) % max(1, number_of - fixed)
        return jnp.zeros((number_of,), jnp.int32).at[order[jnp.where(places < fixed, places, passed)]].set(jnp.asarray(sizes, jnp.int32))

    sizes = jnp.where(number % 4 == 0, named(crowded, number // 4), named(usual, number - number // 4 - 1))
    mixed = jax.random.permutation(jax.random.fold_in(own, 3), number_of)
    donor, sink = mixed[0:number_of // 2 * 2:2], mixed[1:number_of // 2 * 2:2]
    slack = jnp.minimum(sizes[donor] - 1, limit - sizes[sink]) // 2
    slack = jnp.where((donor == order[0]) | (sink == order[0]) | (sizes[sink] == 0), 0, jnp.maximum(slack, 0))
    passed = jax.random.randint(jax.random.fold_in(own, 4), (number_of // 2,), 0, 1 << 20) % (slack + 1)
    sizes = sizes.at[donor].add(-passed).at[sink].add(passed)
    members = jnp.searchsorted(jnp.cumsum(sizes), jnp.arange(rows * top), side="right").astype(jnp.int32)
    table = members.reshape(top, rows).T
    table = table[jax.random.permutation(jax.random.fold_in(own, 1), rows)]
    offset_by = jax.random.randint(jax.random.fold_in(own, 2), (rows, 1), 0, top)
    return jnp.take_along_axis(table, (jnp.arange(top)[None, :] + offset_by) % top, axis=1)


def load_shares(amount, total, most, lean, full):
    portions = [(1 << 20) // math.isqrt(grade ** lean) + 1 for grade in range(1, amount + 1)]
    largest = most if full else min(most, max(-(-total // amount), total * portions[0] // sum(portions)))
    least = 1 if total - largest >= amount - 1 else 0
    holding, surplus = [largest] + [least] * (amount - 1), total - largest - least * (amount - 1)
    while surplus > 0:
        movable = [i for i in range(1, amount) if holding[i] < largest] or [i for i in range(1, amount) if holding[i] < most]
        whole, left = sum([portions[i] for i in movable]), surplus
        for i in movable:
            more = min(most - holding[i], max(1, left * portions[i] // whole), surplus)
            holding[i] = holding[i] + more
            surplus = surplus - more
    return np.array(holding)


def normal_values(own_key, extent, spread, limit, cuts=(), kind=jnp.bfloat16):
    result = spread * jax.random.normal(own_key, extent, jnp.float32)
    if cuts:
        result = result * shard_levels(own_key, extent, cuts, -0.22, 0.18)
    return jnp.clip(result, -limit, limit).astype(kind)


def setup_inputs(seed: int = 0, part: int = 0) -> dict:
    streams_of = jax.random.split(jax.random.key(seed), 9)
    part_splits = jax.random.split(jax.random.fold_in(streams_of[8], part), 9)
    tokens = normal_values(part_splits[0], (TOKENS, D), 1.0, 6.0, ((0, 16),))
    expert_ids_keys = jax.random.split(jax.random.fold_in(part_splits[1], 1), TOKENS // TOK_DEV)
    expert_ids_turns = jax.random.permutation(jax.random.fold_in(part_splits[1], 3), TOKENS // TOK_DEV)
    expert_ids = jax.vmap(lambda own, number: deal_out(jax.random.fold_in(part_splits[1], 2), own, number, TOK_DEV, EXPERTS, TOPK, CAP, 2))(expert_ids_keys, expert_ids_turns).reshape((TOKENS, TOPK))
    keep_flags = touch_ends((jax.random.randint(part_splits[2], (TOKENS, TOPK), 0, 8) < 7).astype(jnp.int32), jax.random.fold_in(part_splits[2], 1), 0, 1)
    router_weights = jnp.clip(jnp.exp(math.log(1.0) - 2.9957323 * jax.random.uniform(part_splits[3], (TOKENS, TOPK), jnp.float32) ** shard_levels(part_splits[3], (TOKENS, TOPK), ((0, 16),), -0.2, 0.2)), 0.05, 1.0)
    grad_out = normal_values(part_splits[4], (TOKENS, D), 1.0, 6.0, ((0, 16),))
    gate_weight = normal_values(streams_of[5], (EXPERTS, D, HID), D ** -0.5, 0.125, ((0, 16),))
    up_weight = normal_values(streams_of[6], (EXPERTS, D, HID), D ** -0.5, 0.125, ((0, 16),))
    down_weight = normal_values(streams_of[7], (EXPERTS, HID, D), HID ** -0.5, 0.21875, ((0, 16),))
    return {"tokens": tokens, "expert_ids": expert_ids, "keep_flags": keep_flags, "router_weights": router_weights, "grad_out": grad_out, "gate_weight": gate_weight, "up_weight": up_weight, "down_weight": down_weight}


def silu_parts(gate_pre):
    sigmoid_gate = jax.nn.sigmoid(gate_pre)
    return gate_pre * sigmoid_gate, sigmoid_gate


def reference(tokens, expert_ids, keep_flags, router_weights, grad_out, gate_weight, up_weight, down_weight):
    per_block = TOK_DEV * TOPK
    slot_count = N_EXPERT * CAP
    slot_total = EXPERTS * slot_count
    hid_part = HID // HID_BLOCKS
    block_ids = expert_ids.reshape(N_EXPERT, per_block)
    onehot = (block_ids[:, :, None] == jnp.arange(EXPERTS, dtype=jnp.int32)[None, None, :]).astype(jnp.int32)
    before = jnp.cumsum(onehot, axis=1) - onehot
    slot_rank = jnp.sum(before * onehot, axis=2)
    source_block = jnp.arange(N_EXPERT, dtype=jnp.int32)[:, None]
    target = ((block_ids * N_EXPERT + source_block) * CAP + slot_rank).reshape(-1).astype(jnp.int32)
    token_index = (jnp.arange(TOKENS * TOPK, dtype=jnp.int32) // TOPK).astype(jnp.int32)
    keep_float = keep_flags.astype(jnp.float32)
    scale = keep_float * router_weights
    tok_of = jnp.zeros((slot_total,), jnp.int32).at[target].set(token_index)
    live_of = jnp.zeros((slot_total,), jnp.float32).at[target].set(keep_float.reshape(-1))
    scale_of = jnp.zeros((slot_total,), jnp.float32).at[target].set(scale.reshape(-1))

    def one_expert(expert):
        start = (expert * slot_count).astype(jnp.int32)
        source_rows = lax.dynamic_slice_in_dim(tok_of, start, slot_count)
        live_rows = lax.dynamic_slice_in_dim(live_of, start, slot_count)
        scale_rows = lax.dynamic_slice_in_dim(scale_of, start, slot_count)
        received = (tokens[source_rows].astype(jnp.float32) * live_rows[:, None]).astype(jnp.bfloat16)
        gate_mat = gate_weight[expert]
        up_mat = up_weight[expert]
        down_mat = down_weight[expert]
        gate_pre = jnp.dot(received, gate_mat, preferred_element_type=jnp.float32)
        up_pre = jnp.dot(received, up_mat, preferred_element_type=jnp.float32)
        activated, sigmoid_gate = silu_parts(gate_pre)
        hidden = (activated * up_pre).astype(jnp.bfloat16)
        out_sum = jnp.zeros((slot_count, D), jnp.float32)
        for block in range(HID_BLOCKS):
            lower = block * hid_part
            upper = lower + hid_part
            piece = jnp.dot(hidden[:, lower:upper], down_mat[lower:upper], preferred_element_type=jnp.float32).astype(jnp.bfloat16)
            out_sum = out_sum + lax.optimization_barrier(piece).astype(jnp.float32)
        expert_out = out_sum.astype(jnp.bfloat16)
        grad_rows = (scale_rows[:, None] * grad_out[source_rows].astype(jnp.float32)).astype(jnp.bfloat16)
        grad_hidden = jnp.dot(grad_rows, down_mat.T, preferred_element_type=jnp.float32)
        grad_gate = (grad_hidden * up_pre * sigmoid_gate * (1.0 + gate_pre * (1.0 - sigmoid_gate))).astype(jnp.bfloat16)
        grad_up = (grad_hidden * activated).astype(jnp.bfloat16)
        grad_sum = jnp.zeros((slot_count, D), jnp.float32)
        for block in range(HID_BLOCKS):
            lower = block * hid_part
            upper = lower + hid_part
            piece = jnp.dot(grad_gate[:, lower:upper], gate_mat[:, lower:upper].T, preferred_element_type=jnp.float32)
            piece = piece + jnp.dot(grad_up[:, lower:upper], up_mat[:, lower:upper].T, preferred_element_type=jnp.float32)
            grad_sum = grad_sum + lax.optimization_barrier(piece.astype(jnp.bfloat16)).astype(jnp.float32)
        return expert_out, grad_sum.astype(jnp.bfloat16)

    expert_outs, expert_grads = lax.map(one_expert, jnp.arange(EXPERTS, dtype=jnp.int32))
    out_assign = expert_outs.reshape(slot_total, D)[target].astype(jnp.float32).reshape(TOKENS, TOPK, D)
    combined = jnp.sum(scale[:, :, None] * out_assign, axis=1).astype(jnp.bfloat16)
    grad_weights = keep_float * jnp.sum(grad_out.astype(jnp.float32)[:, None, :] * out_assign, axis=2)
    grad_assign = expert_grads.reshape(slot_total, D)[target].astype(jnp.float32).reshape(TOKENS, TOPK, D)
    grad_tokens = jnp.sum(grad_assign, axis=1).astype(jnp.bfloat16)
    return combined, grad_tokens, grad_weights
```

```python
import functools

import jax
import jax.numpy as jnp
from jax import lax
from jax.experimental import pallas as pl
from jax.experimental.pallas import tpu as pltpu
from jax.sharding import PartitionSpec as P

LANES = 128
MESH_ID = pl.DeviceIdType.MESH


def route_tables(expert_ids, keep_flags, experts, capacity):
    tok_count, top_count = expert_ids.shape
    flat_ids = expert_ids.reshape(tok_count * top_count)
    onehot = (flat_ids[:, None] == jnp.arange(experts, dtype=jnp.int32)[None, :]).astype(jnp.int32)
    before = jnp.cumsum(onehot, axis=0) - onehot
    slot_rank = jnp.sum(before * onehot, axis=1)
    target = flat_ids * capacity + slot_rank
    picker = target[:, None] == jnp.arange(experts * capacity, dtype=jnp.int32)[None, :]
    kept = keep_flags.reshape(tok_count * top_count)[:, None] > 0
    sender = jnp.sum(
        (picker & kept).astype(jnp.bfloat16).reshape(tok_count, top_count, experts * capacity),
        axis=1,
    )
    return (picker.astype(jnp.bfloat16), sender)


def pack_rows(sender, source_cols, experts, capacity):
    packed = jnp.einsum("ts,td->sd", sender, source_cols, preferred_element_type=jnp.float32)
    return packed.astype(jnp.bfloat16).reshape(experts, capacity, source_cols.shape[1])


def local_exchange(
    tokens, expert_ids, keep_flags, router_weights, grad_out, gate_weight, up_weight, down_weight
):
    experts = lax.axis_size("expert")
    tok_count, top_count = expert_ids.shape
    capacity = min(tok_count, max(2, 2 * tok_count * top_count // experts))
    width = tokens.shape[1]
    width_half = grad_out.shape[1]
    gate_mat = gate_weight[0]
    up_mat = up_weight[0]
    down_mat = down_weight[0]
    picker, sender = route_tables(expert_ids, keep_flags, experts, capacity)
    keep_float = keep_flags.astype(jnp.float32)
    scale = keep_float * router_weights
    packed = pack_rows(sender, tokens, experts, capacity)
    received = lax.all_to_all(packed, "expert", split_axis=0, concat_axis=0, tiled=True)
    gate_pre = jnp.einsum("scd,dh->sch", received, gate_mat, preferred_element_type=jnp.float32)
    up_pre = jnp.einsum("scd,dh->sch", received, up_mat, preferred_element_type=jnp.float32)
    hidden = (jax.nn.silu(gate_pre) * up_pre).astype(jnp.bfloat16)
    partials = jnp.einsum("sch,hd->scd", hidden, down_mat, preferred_element_type=jnp.float32)
    partials, gate_pre, up_pre = (partials, gate_pre, up_pre)
    out_half = lax.psum_scatter(
        partials.astype(jnp.bfloat16), "tensor", scatter_dimension=2, tiled=True
    )
    returned = lax.all_to_all(out_half, "expert", split_axis=0, concat_axis=0, tiled=True).reshape(
        experts * capacity, width_half
    )
    out_assign = jnp.dot(picker, returned, preferred_element_type=jnp.float32).reshape(
        tok_count, top_count, width_half
    )
    combined = jnp.sum(scale[:, :, None] * out_assign, axis=1).astype(jnp.bfloat16)
    grad_float = grad_out.astype(jnp.float32)
    local_dots = keep_float * jnp.sum(grad_float[:, None, :] * out_assign, axis=2)
    grad_weights = lax.psum(local_dots, "tensor")
    grad_full = lax.all_gather(grad_out, "tensor", axis=1, tiled=True)
    grad_assign = (scale[:, :, None] * grad_full.astype(jnp.float32)[:, None, :]).astype(
        jnp.bfloat16
    )
    grad_assign = grad_assign.reshape(tok_count * top_count, width)
    grad_packed = jnp.einsum("as,ad->sd", picker, grad_assign, preferred_element_type=jnp.float32)
    grad_packed = grad_packed.astype(jnp.bfloat16).reshape(experts, capacity, width)
    grad_rows = lax.all_to_all(grad_packed, "expert", split_axis=0, concat_axis=0, tiled=True)
    grad_hidden = jnp.einsum("scd,hd->sch", grad_rows, down_mat, preferred_element_type=jnp.float32)
    sigmoid_gate = jax.nn.sigmoid(gate_pre)
    activated = gate_pre * sigmoid_gate
    grad_gate = (
        grad_hidden * up_pre * sigmoid_gate * (1.0 + gate_pre * (1.0 - sigmoid_gate))
    ).astype(jnp.bfloat16)
    grad_up = (grad_hidden * activated).astype(jnp.bfloat16)
    grad_part = jnp.einsum("sch,dh->scd", grad_gate, gate_mat, preferred_element_type=jnp.float32)
    grad_part = grad_part + jnp.einsum(
        "sch,dh->scd", grad_up, up_mat, preferred_element_type=jnp.float32
    )
    grad_half = lax.psum_scatter(
        grad_part.astype(jnp.bfloat16), "tensor", scatter_dimension=2, tiled=True
    )
    grad_back = lax.all_to_all(
        grad_half, "expert", split_axis=0, concat_axis=0, tiled=True
    ).reshape(experts * capacity, width_half)
    grad_picked = jnp.dot(picker, grad_back, preferred_element_type=jnp.float32).reshape(
        tok_count, top_count, width_half
    )
    grad_tokens = jnp.sum(grad_picked, axis=1).astype(jnp.bfloat16)
    return (combined, grad_tokens, grad_weights)


def fused_kernel(depth, chunk, tokens, ids, keep, weights, cotangent, gate_hbm, up_hbm, down_hbm,
                 combined, grad_tokens, grad_weights, rows, grads, gate_w, up_w, down_w, act, slope,
                 hidden, d_gate, d_up, *rest):
    count = len(chunk)
    part, from_core, to_side, from_side, total, from_line = (
        rest[i * count:(i + 1) * count] for i in range(6)
    )
    (w_sem, line_s, line_r, side_s, side_r, core_s, core_r,
     a_s, a_r, b_s, b_r, c_s, c_r) = rest[6 * count:]
    experts = lax.axis_size("expert")
    me = lax.axis_index("expert")
    core, side, line = lax.rem(me, 2), lax.rem(me // 2, 2), me // 4
    tok_count, width = tokens.shape
    hid = hidden.shape[1]
    total_rows = 4 * depth * tok_count

    def device(z, x, c):
        return {"expert": (z * 2 + x) * 2 + c}

    def behind(step):
        return lax.rem(line + depth - step, depth)

    def ahead(step):
        return lax.rem(line + step, depth)

    barrier = pltpu.get_barrier_semaphore()
    peers = [device(ahead(step), side, core) for step in range(1, depth)]
    side_peer = device(line, 1 - side, core)
    core_peer = device(line, side, 1 - core)
    for peer in peers + [side_peer, core_peer]:
        pl.semaphore_signal(barrier, inc=1, device_id=peer, device_id_type=MESH_ID)

    loads = [
        pltpu.make_async_copy(source, target, w_sem.at[i])
        for i, (source, target) in enumerate(
            ((gate_hbm.at[0], gate_w), (up_hbm.at[0], up_w), (down_hbm.at[0], down_w))
        )
    ]
    for load in loads:
        load.start()

    lane = lax.broadcasted_iota(jnp.int32, (tok_count, LANES), 1)
    scale_own = jnp.zeros((tok_count, LANES), jnp.float32)
    own_scale = keep[...].astype(jnp.float32) * weights[...]
    for k in range(ids.shape[1]):
        hit = lax.rem(lane, experts) == ids[:, k:k + 1]
        scale_own = jnp.where(hit, own_scale[:, k:k + 1], scale_own)
    high = scale_own.astype(jnp.bfloat16).astype(jnp.float32)
    coded = jnp.where(lane < experts, high, scale_own - high)
    coded = jnp.where(lane < 2 * experts, coded, 0.0)
    rows[core, side, line, :, :width] = tokens[...]
    rows[core, side, line, :, width:] = coded.astype(jnp.bfloat16)
    grads[core, side, line] = cotangent[...]

    pl.semaphore_wait(barrier, depth + 1)

    sent = []

    def send(source, target, s_sem, r_sem, peer):
        copy = pltpu.make_async_remote_copy(
            src_ref=source, dst_ref=target, send_sem=s_sem, recv_sem=r_sem,
            device_id=peer, device_id_type=MESH_ID,
        )
        copy.start()
        sent.append(copy)

    def arrive(target, s_sem, r_sem, peer):
        pltpu.make_async_remote_copy(
            src_ref=target, dst_ref=target, send_sem=s_sem, recv_sem=r_sem,
            device_id=peer, device_id_type=MESH_ID,
        ).wait_recv()

    def share_step(buf, which, step):
        block = buf.at[core, side, behind(step)]
        send(block, block, side_s.at[which, step], side_r.at[which, step], side_peer)
        send(block, block, core_s.at[which, step], core_r.at[which, step], core_peer)

    def gather_start(buf, which):
        block = buf.at[core, side, line]
        for step in range(1, depth):
            send(block, block, line_s.at[which, step], line_r.at[which, step], peers[step - 1])
        share_step(buf, which, 0)

    def gather_line(buf, which):
        for step in range(1, depth):
            arrive(buf.at[core, side, behind(step)], line_s.at[which, step],
                   line_r.at[which, step], peers[step - 1])
            share_step(buf, which, step)

    def gather_side(buf, which):
        for step in range(depth):
            block = buf.at[core, 1 - side, behind(step)]
            arrive(block, side_s.at[which, step], side_r.at[which, step], side_peer)
            send(block, block, core_s.at[which, depth + step], core_r.at[which, depth + step],
                 core_peer)

    def gather_end(buf, which):
        for step in range(2 * depth):
            x = side if step < depth else 1 - side
            arrive(buf.at[1 - core, x, behind(step % depth)], core_s.at[which, step],
                   core_r.at[which, step], core_peer)

    gather_start(rows, 0)
    gather_line(rows, 0)
    gather_start(grads, 1)
    gather_side(rows, 0)
    gather_end(rows, 0)
    loads[0].wait()
    loads[1].wait()

    tile = 256
    data = rows[:, :, :, :, :width].reshape(total_rows, width)
    lanes = lax.broadcasted_iota(jnp.int32, (total_rows, LANES), 1)
    coded_all = rows[:, :, :, :, width:].reshape(total_rows, LANES).astype(jnp.float32)
    mine = lax.rem(lanes, experts) == me
    scale = jnp.sum(jnp.where(mine, coded_all, 0.0), axis=1, keepdims=True)

    for t in range(hid // tile):
        cols = slice(t * tile, (t + 1) * tile)
        gate = jnp.dot(data, gate_w[:, cols], preferred_element_type=jnp.float32)
        up = jnp.dot(data, up_w[:, cols], preferred_element_type=jnp.float32)
        sig = jax.nn.sigmoid(gate)
        activated = gate * sig
        act[:, cols] = activated
        slope[:, cols] = up * sig * (1.0 + gate * (1.0 - sig))
        hidden[:, cols] = (activated * up).astype(jnp.bfloat16)
        if t == 0:
            gather_line(grads, 1)

    def send_core(q):
        send(part[q].at[1 - core], from_core[q], a_s.at[q], a_r.at[q], core_peer)

    def send_side(q):
        arrive(from_core[q], a_s.at[q], a_r.at[q], core_peer)
        away = part[q][core, 1 - side].astype(jnp.float32)
        away = away + from_core[q][1 - side].astype(jnp.float32)
        to_side[q][...] = away.astype(jnp.bfloat16)
        send(to_side[q], from_side[q], b_s.at[q], b_r.at[q], side_peer)

    def send_line(q):
        arrive(from_side[q], b_s.at[q], b_r.at[q], side_peer)
        for step in range(1, depth):
            z = ahead(step)
            block = part[q][core, side, z].astype(jnp.float32)
            block = block + from_core[q][side, z].astype(jnp.float32)
            block = block + from_side[q][z].astype(jnp.float32)
            total[q][step] = block.astype(jnp.bfloat16)
            send(total[q].at[step], from_line[q].at[step], c_s.at[q, step], c_r.at[q, step],
                 peers[step - 1])

    def finish(q):
        block = part[q][core, side, line].astype(jnp.float32)
        block = block + from_core[q][side, line].astype(jnp.float32)
        block = block + from_side[q][line].astype(jnp.float32)
        for step in range(1, depth):
            arrive(from_line[q].at[step], c_s.at[q, step], c_r.at[q, step], peers[step - 1])
            block = block + from_line[q][step].astype(jnp.float32)
        return block

    half = count // 2
    cuts = []
    at = 0
    for q in range(half):
        cuts.append(slice(at, at + chunk[q]))
        at += chunk[q]
    shape = (2, 2, depth, tok_count)
    loads[2].wait()
    for q in range(half):
        out = jnp.dot(hidden[...], down_w[:, cuts[q]], preferred_element_type=jnp.float32)
        out = (scale * out).astype(jnp.bfloat16)
        part[q][...] = out.reshape(shape + (chunk[q],))
        send_core(q)
        if q >= 1:
            send_side(q - 1)
    gather_side(grads, 1)
    send_side(half - 1)
    gather_end(grads, 1)

    grad_data = grads[...].reshape(total_rows, width)
    dots = jnp.zeros((total_rows, 1), jnp.float32)
    contract = (((1,), (1,)), ((), ()))
    for t in range(hid // tile):
        cols = slice(t * tile, (t + 1) * tile)
        back = lax.dot_general(grad_data, down_w[cols, :], contract,
                               preferred_element_type=jnp.float32)
        dots = dots + jnp.sum(back * hidden[:, cols].astype(jnp.float32), axis=1, keepdims=True)
        back = back * scale
        d_gate[:, cols] = (back * slope[:, cols]).astype(jnp.bfloat16)
        d_up[:, cols] = (back * act[:, cols]).astype(jnp.bfloat16)
    dots_high = dots.astype(jnp.bfloat16).astype(jnp.float32)
    dots_coded = jnp.where(lanes < experts, dots_high, dots - dots_high)
    dots_coded = jnp.where(mine & (lanes < 2 * experts), dots_coded, 0.0).astype(jnp.bfloat16)

    for i in range(half):
        q = half + i
        wide = chunk[i]
        grad = lax.dot_general(d_gate[...], gate_w[cuts[i], :], contract,
                               preferred_element_type=jnp.float32)
        grad = grad + lax.dot_general(d_up[...], up_w[cuts[i], :], contract,
                                      preferred_element_type=jnp.float32)
        part[q][:, :, :, :, :wide] = grad.astype(jnp.bfloat16).reshape(shape + (wide,))
        if i == 0:
            part[q][:, :, :, :, wide:] = dots_coded.reshape(shape + (LANES,))
        send_core(q)
        if i >= 1:
            send_side(q - 1)
        send_line(i)
    send_side(count - 1)
    for q in range(half, count):
        send_line(q)
    for q in range(half):
        combined[:, cuts[q]] = finish(q).astype(jnp.bfloat16)
    for i in range(half):
        block = finish(half + i)
        grad_tokens[:, cuts[i]] = block[:, :chunk[i]].astype(jnp.bfloat16)
        if i == 0:
            tail = block[:, chunk[i]:]
            tail = jnp.where(lane < 2 * experts, tail, 0.0)
            for k in range(ids.shape[1]):
                hit = lax.rem(lane, experts) == ids[:, k:k + 1]
                picked = jnp.sum(jnp.where(hit, tail, 0.0), axis=1, keepdims=True)
                grad_weights[:, k:k + 1] = keep[:, k:k + 1].astype(jnp.float32) * picked
    for copy in sent:
        copy.wait_send()


def local_fused(
    tokens, expert_ids, keep_flags, router_weights, grad_out, gate_weight, up_weight, down_weight
):
    depth = lax.axis_size("expert") // 4
    tok_count, width = tokens.shape
    hid = gate_weight.shape[2]
    total_rows = 4 * depth * tok_count
    pieces = 4
    each = width // pieces
    chunk = [each] * (2 * pieces)
    chunk[pieces] += LANES
    bf16, f32 = jnp.bfloat16, jnp.float32

    def blocks(*lead):
        return [pltpu.VMEM(lead + (tok_count, wide), bf16) for wide in chunk]

    scratch = [
        pltpu.VMEM((2, 2, depth, tok_count, width + LANES), bf16),
        pltpu.VMEM((2, 2, depth, tok_count, width), bf16),
        pltpu.VMEM(gate_weight.shape[1:], bf16),
        pltpu.VMEM(up_weight.shape[1:], bf16),
        pltpu.VMEM(down_weight.shape[1:], bf16),
        pltpu.VMEM((total_rows, hid), f32),
        pltpu.VMEM((total_rows, hid), f32),
        pltpu.VMEM((total_rows, hid), bf16),
        pltpu.VMEM((total_rows, hid), bf16),
        pltpu.VMEM((total_rows, hid), bf16),
        *blocks(2, 2, depth),
        *blocks(2, depth),
        *blocks(depth),
        *blocks(depth),
        *blocks(depth),
        *blocks(depth),
    ]
    sems = [(3,)] + [(2, depth)] * 4 + [(2, 2 * depth)] * 2
    sems += [(len(chunk),)] * 4 + [(len(chunk), depth)] * 2
    scratch += [pltpu.SemaphoreType.DMA(dims) for dims in sems]
    vmem = pl.BlockSpec(memory_space=pltpu.VMEM)
    far = pl.BlockSpec(memory_space=pl.ANY)
    return pl.pallas_call(
        functools.partial(fused_kernel, depth, chunk),
        out_shape=(
            jax.ShapeDtypeStruct(tokens.shape, bf16),
            jax.ShapeDtypeStruct(tokens.shape, bf16),
            jax.ShapeDtypeStruct(router_weights.shape, f32),
        ),
        in_specs=[vmem] * 5 + [far] * 3,
        out_specs=(vmem, vmem, vmem),
        scratch_shapes=scratch,
        compiler_params=pltpu.CompilerParams(
            collective_id=0, has_side_effects=True, vmem_limit_bytes=56 * 1024 * 1024
        ),
        cost_estimate=pl.CostEstimate(
            flops=12 * total_rows * width * hid,
            bytes_accessed=6 * width * hid,
            transcendentals=total_rows * hid,
        ),
    )(tokens, expert_ids, keep_flags, router_weights, grad_out, gate_weight, up_weight, down_weight)


def solution(mesh):
    sizes = mesh.shape
    dense = sizes["tensor"] == 1 and sizes["expert"] % 4 == 0 and 8 <= sizes["expert"] <= 32
    local = local_fused if dense else local_exchange
    in_specs = (
        P(("groups", "expert"), None),
        P(("groups", "expert"), None),
        P(("groups", "expert"), None),
        P(("groups", "expert"), None),
        P(("groups", "expert"), "tensor"),
        P("expert", None, "tensor"),
        P("expert", None, "tensor"),
        P("expert", "tensor", None),
    )
    out_specs = (
        P(("groups", "expert"), "tensor"),
        P(("groups", "expert"), "tensor"),
        P(("groups", "expert"), None),
    )
    return jax.shard_map(local, mesh=mesh, in_specs=in_specs, out_specs=out_specs, check_vma=False)
```

```python
import functools

import jax
import jax.numpy as jnp
from jax import lax
from jax.experimental import pallas as pl
from jax.experimental.pallas import tpu as pltpu
from jax.sharding import PartitionSpec as P

LANES = 128
MESH_ID = pl.DeviceIdType.MESH


def route_tables(expert_ids, keep_flags, experts, capacity):
    tok_count, top_count = expert_ids.shape
    flat_ids = expert_ids.reshape(tok_count * top_count)
    onehot = (flat_ids[:, None] == jnp.arange(experts, dtype=jnp.int32)[None, :]).astype(jnp.int32)
    before = jnp.cumsum(onehot, axis=0) - onehot
    slot_rank = jnp.sum(before * onehot, axis=1)
    target = flat_ids * capacity + slot_rank
    picker = target[:, None] == jnp.arange(experts * capacity, dtype=jnp.int32)[None, :]
    kept = keep_flags.reshape(tok_count * top_count)[:, None] > 0
    sender = jnp.sum(
        (picker & kept).astype(jnp.bfloat16).reshape(tok_count, top_count, experts * capacity),
        axis=1,
    )
    return (picker.astype(jnp.bfloat16), sender)


def pack_rows(sender, source_cols, experts, capacity):
    packed = jnp.einsum("ts,td->sd", sender, source_cols, preferred_element_type=jnp.float32)
    return packed.astype(jnp.bfloat16).reshape(experts, capacity, source_cols.shape[1])


def local_exchange(
    tokens, expert_ids, keep_flags, router_weights, grad_out, gate_weight, up_weight, down_weight
):
    experts = lax.axis_size("expert")
    tok_count, top_count = expert_ids.shape
    capacity = min(tok_count, max(2, 2 * tok_count * top_count // experts))
    width = tokens.shape[1]
    width_half = grad_out.shape[1]
    gate_mat = gate_weight[0]
    up_mat = up_weight[0]
    down_mat = down_weight[0]
    picker, sender = route_tables(expert_ids, keep_flags, experts, capacity)
    keep_float = keep_flags.astype(jnp.float32)
    scale = keep_float * router_weights
    packed = pack_rows(sender, tokens, experts, capacity)
    received = lax.all_to_all(packed, "expert", split_axis=0, concat_axis=0, tiled=True)
    gate_pre = jnp.einsum("scd,dh->sch", received, gate_mat, preferred_element_type=jnp.float32)
    up_pre = jnp.einsum("scd,dh->sch", received, up_mat, preferred_element_type=jnp.float32)
    hidden = (jax.nn.silu(gate_pre) * up_pre).astype(jnp.bfloat16)
    partials = jnp.einsum("sch,hd->scd", hidden, down_mat, preferred_element_type=jnp.float32)
    partials, gate_pre, up_pre = (partials, gate_pre, up_pre)
    out_half = lax.psum_scatter(
        partials.astype(jnp.bfloat16), "tensor", scatter_dimension=2, tiled=True
    )
    returned = lax.all_to_all(out_half, "expert", split_axis=0, concat_axis=0, tiled=True).reshape(
        experts * capacity, width_half
    )
    out_assign = jnp.dot(picker, returned, preferred_element_type=jnp.float32).reshape(
        tok_count, top_count, width_half
    )
    combined = jnp.sum(scale[:, :, None] * out_assign, axis=1).astype(jnp.bfloat16)
    grad_float = grad_out.astype(jnp.float32)
    local_dots = keep_float * jnp.sum(grad_float[:, None, :] * out_assign, axis=2)
    grad_weights = lax.psum(local_dots, "tensor")
    grad_full = lax.all_gather(grad_out, "tensor", axis=1, tiled=True)
    grad_assign = (scale[:, :, None] * grad_full.astype(jnp.float32)[:, None, :]).astype(
        jnp.bfloat16
    )
    grad_assign = grad_assign.reshape(tok_count * top_count, width)
    grad_packed = jnp.einsum("as,ad->sd", picker, grad_assign, preferred_element_type=jnp.float32)
    grad_packed = grad_packed.astype(jnp.bfloat16).reshape(experts, capacity, width)
    grad_rows = lax.all_to_all(grad_packed, "expert", split_axis=0, concat_axis=0, tiled=True)
    grad_hidden = jnp.einsum("scd,hd->sch", grad_rows, down_mat, preferred_element_type=jnp.float32)
    sigmoid_gate = jax.nn.sigmoid(gate_pre)
    activated = gate_pre * sigmoid_gate
    grad_gate = (
        grad_hidden * up_pre * sigmoid_gate * (1.0 + gate_pre * (1.0 - sigmoid_gate))
    ).astype(jnp.bfloat16)
    grad_up = (grad_hidden * activated).astype(jnp.bfloat16)
    grad_part = jnp.einsum("sch,dh->scd", grad_gate, gate_mat, preferred_element_type=jnp.float32)
    grad_part = grad_part + jnp.einsum(
        "sch,dh->scd", grad_up, up_mat, preferred_element_type=jnp.float32
    )
    grad_half = lax.psum_scatter(
        grad_part.astype(jnp.bfloat16), "tensor", scatter_dimension=2, tiled=True
    )
    grad_back = lax.all_to_all(
        grad_half, "expert", split_axis=0, concat_axis=0, tiled=True
    ).reshape(experts * capacity, width_half)
    grad_picked = jnp.dot(picker, grad_back, preferred_element_type=jnp.float32).reshape(
        tok_count, top_count, width_half
    )
    grad_tokens = jnp.sum(grad_picked, axis=1).astype(jnp.bfloat16)
    return (combined, grad_tokens, grad_weights)


def fused_kernel(depth, chunk, tokens, ids, keep, weights, cotangent, gate_hbm, up_hbm, down_hbm,
                 combined, grad_tokens, grad_weights, rows, grads, gate_w, up_w, down_w, act, slope,
                 hidden, d_gate, d_up, *rest):
    count = len(chunk)
    part, from_core, to_side, from_side, total, from_line = (
        rest[i * count:(i + 1) * count] for i in range(6)
    )
    (w_sem, line_s, line_r, side_s, side_r, core_s, core_r,
     a_s, a_r, b_s, b_r, c_s, c_r) = rest[6 * count:]
    experts = lax.axis_size("expert")
    me = lax.axis_index("expert")
    core, side, line = lax.rem(me, 2), lax.rem(me // 2, 2), me // 4
    tok_count, width = tokens.shape
    hid = hidden.shape[1]
    total_rows = 4 * depth * tok_count

    def device(z, x, c):
        return {"expert": (z * 2 + x) * 2 + c}

    def behind(step):
        return lax.rem(line + depth - step, depth)

    def ahead(step):
        return lax.rem(line + step, depth)

    barrier = pltpu.get_barrier_semaphore()
    peers = [device(ahead(step), side, core) for step in range(1, depth)]
    side_peer = device(line, 1 - side, core)
    core_peer = device(line, side, 1 - core)
    for peer in peers + [side_peer, core_peer]:
        pl.semaphore_signal(barrier, inc=1, device_id=peer, device_id_type=MESH_ID)

    loads = [
        pltpu.make_async_copy(source, target, w_sem.at[i])
        for i, (source, target) in enumerate(
            ((gate_hbm.at[0], gate_w), (up_hbm.at[0], up_w), (down_hbm.at[0], down_w))
        )
    ]
    for load in loads:
        load.start()

    lane = lax.broadcasted_iota(jnp.int32, (tok_count, LANES), 1)
    place = lax.rem(lax.broadcasted_iota(jnp.int32, (LANES, tok_count), 0), experts)
    own_scale = keep[...].astype(jnp.float32) * weights[...]
    scale_own = jnp.zeros((LANES, tok_count), jnp.float32)
    for k in range(ids.shape[0]):
        scale_own = jnp.where(place == ids[k:k + 1, :], own_scale[k:k + 1, :], scale_own)
    scale_own = scale_own.T
    high = scale_own.astype(jnp.bfloat16).astype(jnp.float32)
    coded = jnp.where(lane < experts, high, scale_own - high)
    coded = jnp.where(lane < 2 * experts, coded, 0.0)
    rows[core, side, line, :, :width] = tokens[...]
    rows[core, side, line, :, width:] = coded.astype(jnp.bfloat16)
    grads[core, side, line] = cotangent[...]

    pl.semaphore_wait(barrier, depth + 1)

    sent = []

    def send(source, target, s_sem, r_sem, peer):
        copy = pltpu.make_async_remote_copy(
            src_ref=source, dst_ref=target, send_sem=s_sem, recv_sem=r_sem,
            device_id=peer, device_id_type=MESH_ID,
        )
        copy.start()
        sent.append(copy)

    def arrive(target, s_sem, r_sem, peer):
        pltpu.make_async_remote_copy(
            src_ref=target, dst_ref=target, send_sem=s_sem, recv_sem=r_sem,
            device_id=peer, device_id_type=MESH_ID,
        ).wait_recv()

    def share_step(buf, which, step):
        block = buf.at[core, side, behind(step)]
        send(block, block, side_s.at[which, step], side_r.at[which, step], side_peer)
        send(block, block, core_s.at[which, step], core_r.at[which, step], core_peer)

    def gather_start(buf, which):
        block = buf.at[core, side, line]
        for step in range(1, depth):
            send(block, block, line_s.at[which, step], line_r.at[which, step], peers[step - 1])
        share_step(buf, which, 0)

    def gather_line(buf, which):
        for step in range(1, depth):
            arrive(buf.at[core, side, behind(step)], line_s.at[which, step],
                   line_r.at[which, step], peers[step - 1])
            share_step(buf, which, step)

    def gather_side(buf, which):
        for step in range(depth):
            block = buf.at[core, 1 - side, behind(step)]
            arrive(block, side_s.at[which, step], side_r.at[which, step], side_peer)
            send(block, block, core_s.at[which, depth + step], core_r.at[which, depth + step],
                 core_peer)

    def gather_end(buf, which):
        for step in range(2 * depth):
            x = side if step < depth else 1 - side
            arrive(buf.at[1 - core, x, behind(step % depth)], core_s.at[which, step],
                   core_r.at[which, step], core_peer)

    gather_start(rows, 0)
    gather_line(rows, 0)
    gather_start(grads, 1)
    gather_side(rows, 0)
    gather_end(rows, 0)
    loads[0].wait()
    loads[1].wait()

    tile = 256
    data = rows[:, :, :, :, :width].reshape(total_rows, width)
    lanes = lax.broadcasted_iota(jnp.int32, (total_rows, LANES), 1)
    coded_all = rows[:, :, :, :, width:].reshape(total_rows, LANES).astype(jnp.float32)
    mine = lax.rem(lanes, experts) == me
    scale = jnp.sum(jnp.where(mine, coded_all, 0.0), axis=1, keepdims=True)

    for t in range(hid // tile):
        cols = slice(t * tile, (t + 1) * tile)
        gate = jnp.dot(data, gate_w[:, cols], preferred_element_type=jnp.float32)
        up = jnp.dot(data, up_w[:, cols], preferred_element_type=jnp.float32)
        sig = jax.nn.sigmoid(gate)
        activated = gate * sig
        act[:, cols] = activated
        slope[:, cols] = up * sig * (1.0 + gate * (1.0 - sig))
        hidden[:, cols] = (activated * up).astype(jnp.bfloat16)
        if t == 0:
            gather_line(grads, 1)

    def send_core(q):
        send(part[q].at[1 - core], from_core[q], a_s.at[q], a_r.at[q], core_peer)

    def send_side(q):
        arrive(from_core[q], a_s.at[q], a_r.at[q], core_peer)
        away = part[q][core, 1 - side].astype(jnp.float32)
        away = away + from_core[q][1 - side].astype(jnp.float32)
        to_side[q][...] = away.astype(jnp.bfloat16)
        send(to_side[q], from_side[q], b_s.at[q], b_r.at[q], side_peer)

    def send_line(q):
        arrive(from_side[q], b_s.at[q], b_r.at[q], side_peer)
        for step in range(1, depth):
            z = ahead(step)
            block = part[q][core, side, z].astype(jnp.float32)
            block = block + from_core[q][side, z].astype(jnp.float32)
            block = block + from_side[q][z].astype(jnp.float32)
            total[q][step] = block.astype(jnp.bfloat16)
            send(total[q].at[step], from_line[q].at[step], c_s.at[q, step], c_r.at[q, step],
                 peers[step - 1])

    def finish(q):
        block = part[q][core, side, line].astype(jnp.float32)
        block = block + from_core[q][side, line].astype(jnp.float32)
        block = block + from_side[q][line].astype(jnp.float32)
        for step in range(1, depth):
            arrive(from_line[q].at[step], c_s.at[q, step], c_r.at[q, step], peers[step - 1])
            block = block + from_line[q][step].astype(jnp.float32)
        return block

    half = count // 2
    cuts = []
    at = 0
    for q in range(half):
        cuts.append(slice(at, at + chunk[q]))
        at += chunk[q]
    shape = (2, 2, depth, tok_count)
    loads[2].wait()
    for q in range(half):
        out = jnp.dot(hidden[...], down_w[:, cuts[q]], preferred_element_type=jnp.float32)
        out = (scale * out).astype(jnp.bfloat16)
        part[q][...] = out.reshape(shape + (chunk[q],))
        send_core(q)
        if q >= 1:
            send_side(q - 1)
    gather_side(grads, 1)
    send_side(half - 1)
    gather_end(grads, 1)

    grad_data = grads[...].reshape(total_rows, width)
    dots = jnp.zeros((total_rows, 1), jnp.float32)
    contract = (((1,), (1,)), ((), ()))
    for t in range(hid // tile):
        cols = slice(t * tile, (t + 1) * tile)
        back = lax.dot_general(grad_data, down_w[cols, :], contract,
                               preferred_element_type=jnp.float32)
        dots = dots + jnp.sum(back * hidden[:, cols].astype(jnp.float32), axis=1, keepdims=True)
        back = back * scale
        d_gate[:, cols] = (back * slope[:, cols]).astype(jnp.bfloat16)
        d_up[:, cols] = (back * act[:, cols]).astype(jnp.bfloat16)
    dots_high = dots.astype(jnp.bfloat16).astype(jnp.float32)
    dots_coded = jnp.where(lanes < experts, dots_high, dots - dots_high)
    dots_coded = jnp.where(mine & (lanes < 2 * experts), dots_coded, 0.0).astype(jnp.bfloat16)

    for i in range(half):
        q = half + i
        wide = chunk[i]
        grad = lax.dot_general(d_gate[...], gate_w[cuts[i], :], contract,
                               preferred_element_type=jnp.float32)
        grad = grad + lax.dot_general(d_up[...], up_w[cuts[i], :], contract,
                                      preferred_element_type=jnp.float32)
        part[q][:, :, :, :, :wide] = grad.astype(jnp.bfloat16).reshape(shape + (wide,))
        if i == 0:
            part[q][:, :, :, :, wide:] = dots_coded.reshape(shape + (LANES,))
        send_core(q)
        if i >= 1:
            send_side(q - 1)
        send_line(i)
    send_side(count - 1)
    for q in range(half, count):
        send_line(q)
    for q in range(half):
        combined[:, cuts[q]] = finish(q).astype(jnp.bfloat16)
    for i in range(half):
        block = finish(half + i)
        grad_tokens[:, cuts[i]] = block[:, :chunk[i]].astype(jnp.bfloat16)
        if i == 0:
            tail = block[:, chunk[i]:]
            tail = jnp.where(lane < 2 * experts, tail, 0.0).T
            for k in range(ids.shape[0]):
                picked = jnp.where(place == ids[k:k + 1, :], tail, 0.0)
                picked = jnp.sum(picked, axis=0, keepdims=True)
                grad_weights[k:k + 1, :] = keep[k:k + 1, :].astype(jnp.float32) * picked
    for copy in sent:
        copy.wait_send()


def store_kernel(*refs):
    sem = refs[-1]
    copies = [pltpu.make_async_copy(refs[i], refs[3 + i], sem.at[i]) for i in range(3)]
    for copy in copies:
        copy.start()
    for copy in copies:
        copy.wait()


def local_fused(
    tokens, expert_ids, keep_flags, router_weights, grad_out, gate_weight, up_weight, down_weight
):
    depth = lax.axis_size("expert") // 4
    tok_count, width = tokens.shape
    hid = gate_weight.shape[2]
    total_rows = 4 * depth * tok_count
    pieces = 4
    each = width // pieces
    chunk = [each] * (2 * pieces)
    chunk[pieces] += LANES
    bf16, f32 = jnp.bfloat16, jnp.float32

    def blocks(*lead):
        return [pltpu.VMEM(lead + (tok_count, wide), bf16) for wide in chunk]

    scratch = [
        pltpu.VMEM((2, 2, depth, tok_count, width + LANES), bf16),
        pltpu.VMEM((2, 2, depth, tok_count, width), bf16),
        pltpu.VMEM(gate_weight.shape[1:], bf16),
        pltpu.VMEM(up_weight.shape[1:], bf16),
        pltpu.VMEM(down_weight.shape[1:], bf16),
        pltpu.VMEM((total_rows, hid), f32),
        pltpu.VMEM((total_rows, hid), f32),
        pltpu.VMEM((total_rows, hid), bf16),
        pltpu.VMEM((total_rows, hid), bf16),
        pltpu.VMEM((total_rows, hid), bf16),
        *blocks(2, 2, depth),
        *blocks(2, depth),
        *blocks(depth),
        *blocks(depth),
        *blocks(depth),
        *blocks(depth),
    ]
    sems = [(3,)] + [(2, depth)] * 4 + [(2, 2 * depth)] * 2
    sems += [(len(chunk),)] * 4 + [(len(chunk), depth)] * 2
    scratch += [pltpu.SemaphoreType.DMA(dims) for dims in sems]
    vmem = pl.BlockSpec(memory_space=pltpu.VMEM)
    far = pl.BlockSpec(memory_space=pl.ANY)
    results = pl.pallas_call(
        functools.partial(fused_kernel, depth, chunk),
        out_shape=(
            jax.ShapeDtypeStruct(tokens.shape, bf16),
            jax.ShapeDtypeStruct(tokens.shape, bf16),
            jax.ShapeDtypeStruct(router_weights.shape[::-1], f32),
        ),
        in_specs=[vmem] * 5 + [far] * 3,
        out_specs=(vmem, vmem, vmem),
        scratch_shapes=scratch,
        compiler_params=pltpu.CompilerParams(
            collective_id=0, has_side_effects=True, vmem_limit_bytes=56 * 1024 * 1024
        ),
        cost_estimate=pl.CostEstimate(
            flops=12 * total_rows * width * hid,
            bytes_accessed=6 * width * hid,
            transcendentals=total_rows * hid,
        ),
    )(tokens, expert_ids.T, keep_flags.T, router_weights.T, grad_out, gate_weight, up_weight,
      down_weight)
    combined, grad_tokens, grad_weights = pl.pallas_call(
        store_kernel,
        out_shape=tuple(jax.ShapeDtypeStruct(r.shape, r.dtype) for r in results),
        in_specs=[far] * 3,
        out_specs=(far,) * 3,
        scratch_shapes=[pltpu.SemaphoreType.DMA((3,))],
    )(*results)
    return combined, grad_tokens, grad_weights.T


def solution(mesh):
    sizes = mesh.shape
    dense = sizes["tensor"] == 1 and sizes["expert"] % 4 == 0 and 8 <= sizes["expert"] <= 32
    local = local_fused if dense else local_exchange
    in_specs = (
        P(("groups", "expert"), None),
        P(("groups", "expert"), None),
        P(("groups", "expert"), None),
        P(("groups", "expert"), None),
        P(("groups", "expert"), "tensor"),
        P("expert", None, "tensor"),
        P("expert", None, "tensor"),
        P("expert", "tensor", None),
    )
    out_specs = (
        P(("groups", "expert"), "tensor"),
        P(("groups", "expert"), "tensor"),
        P(("groups", "expert"), None),
    )
    return jax.shard_map(local, mesh=mesh, in_specs=in_specs, out_specs=out_specs, check_vma=False)
```

```python
import functools

import jax
import jax.numpy as jnp
from jax import lax
from jax.experimental import pallas as pl
from jax.experimental.pallas import tpu as pltpu
from jax.sharding import PartitionSpec as P

LANES = 128
MESH_ID = pl.DeviceIdType.MESH


def route_tables(expert_ids, keep_flags, experts, capacity):
    tok_count, top_count = expert_ids.shape
    flat_ids = expert_ids.reshape(tok_count * top_count)
    onehot = (flat_ids[:, None] == jnp.arange(experts, dtype=jnp.int32)[None, :]).astype(jnp.int32)
    before = jnp.cumsum(onehot, axis=0) - onehot
    slot_rank = jnp.sum(before * onehot, axis=1)
    target = flat_ids * capacity + slot_rank
    picker = target[:, None] == jnp.arange(experts * capacity, dtype=jnp.int32)[None, :]
    kept = keep_flags.reshape(tok_count * top_count)[:, None] > 0
    sender = jnp.sum(
        (picker & kept).astype(jnp.bfloat16).reshape(tok_count, top_count, experts * capacity),
        axis=1,
    )
    return (picker.astype(jnp.bfloat16), sender)


def pack_rows(sender, source_cols, experts, capacity):
    packed = jnp.einsum("ts,td->sd", sender, source_cols, preferred_element_type=jnp.float32)
    return packed.astype(jnp.bfloat16).reshape(experts, capacity, source_cols.shape[1])


def local_exchange(
    tokens, expert_ids, keep_flags, router_weights, grad_out, gate_weight, up_weight, down_weight
):
    experts = lax.axis_size("expert")
    tok_count, top_count = expert_ids.shape
    capacity = min(tok_count, max(2, 2 * tok_count * top_count // experts))
    width = tokens.shape[1]
    width_half = grad_out.shape[1]
    gate_mat = gate_weight[0]
    up_mat = up_weight[0]
    down_mat = down_weight[0]
    picker, sender = route_tables(expert_ids, keep_flags, experts, capacity)
    keep_float = keep_flags.astype(jnp.float32)
    scale = keep_float * router_weights
    packed = pack_rows(sender, tokens, experts, capacity)
    received = lax.all_to_all(packed, "expert", split_axis=0, concat_axis=0, tiled=True)
    gate_pre = jnp.einsum("scd,dh->sch", received, gate_mat, preferred_element_type=jnp.float32)
    up_pre = jnp.einsum("scd,dh->sch", received, up_mat, preferred_element_type=jnp.float32)
    hidden = (jax.nn.silu(gate_pre) * up_pre).astype(jnp.bfloat16)
    partials = jnp.einsum("sch,hd->scd", hidden, down_mat, preferred_element_type=jnp.float32)
    partials, gate_pre, up_pre = (partials, gate_pre, up_pre)
    out_half = lax.psum_scatter(
        partials.astype(jnp.bfloat16), "tensor", scatter_dimension=2, tiled=True
    )
    returned = lax.all_to_all(out_half, "expert", split_axis=0, concat_axis=0, tiled=True).reshape(
        experts * capacity, width_half
    )
    out_assign = jnp.dot(picker, returned, preferred_element_type=jnp.float32).reshape(
        tok_count, top_count, width_half
    )
    combined = jnp.sum(scale[:, :, None] * out_assign, axis=1).astype(jnp.bfloat16)
    grad_float = grad_out.astype(jnp.float32)
    local_dots = keep_float * jnp.sum(grad_float[:, None, :] * out_assign, axis=2)
    grad_weights = lax.psum(local_dots, "tensor")
    grad_full = lax.all_gather(grad_out, "tensor", axis=1, tiled=True)
    grad_assign = (scale[:, :, None] * grad_full.astype(jnp.float32)[:, None, :]).astype(
        jnp.bfloat16
    )
    grad_assign = grad_assign.reshape(tok_count * top_count, width)
    grad_packed = jnp.einsum("as,ad->sd", picker, grad_assign, preferred_element_type=jnp.float32)
    grad_packed = grad_packed.astype(jnp.bfloat16).reshape(experts, capacity, width)
    grad_rows = lax.all_to_all(grad_packed, "expert", split_axis=0, concat_axis=0, tiled=True)
    grad_hidden = jnp.einsum("scd,hd->sch", grad_rows, down_mat, preferred_element_type=jnp.float32)
    sigmoid_gate = jax.nn.sigmoid(gate_pre)
    activated = gate_pre * sigmoid_gate
    grad_gate = (
        grad_hidden * up_pre * sigmoid_gate * (1.0 + gate_pre * (1.0 - sigmoid_gate))
    ).astype(jnp.bfloat16)
    grad_up = (grad_hidden * activated).astype(jnp.bfloat16)
    grad_part = jnp.einsum("sch,dh->scd", grad_gate, gate_mat, preferred_element_type=jnp.float32)
    grad_part = grad_part + jnp.einsum(
        "sch,dh->scd", grad_up, up_mat, preferred_element_type=jnp.float32
    )
    grad_half = lax.psum_scatter(
        grad_part.astype(jnp.bfloat16), "tensor", scatter_dimension=2, tiled=True
    )
    grad_back = lax.all_to_all(
        grad_half, "expert", split_axis=0, concat_axis=0, tiled=True
    ).reshape(experts * capacity, width_half)
    grad_picked = jnp.dot(picker, grad_back, preferred_element_type=jnp.float32).reshape(
        tok_count, top_count, width_half
    )
    grad_tokens = jnp.sum(grad_picked, axis=1).astype(jnp.bfloat16)
    return (combined, grad_tokens, grad_weights)


def fused_kernel(depth, chunk, tokens, ids, keep, weights, cotangent, gate_hbm, up_hbm, down_hbm,
                 combined, grad_tokens, grad_weights, rows, grads, gate_w, up_w, down_w, act, slope,
                 hidden, d_gate, d_up, *rest):
    count = len(chunk)
    part, from_core, to_side, from_side, total, from_line = (
        rest[i * count:(i + 1) * count] for i in range(6)
    )
    (w_sem, line_s, line_r, side_s, side_r, core_s, core_r,
     a_s, a_r, b_s, b_r, c_s, c_r) = rest[6 * count:]
    experts = lax.axis_size("expert")
    me = lax.axis_index("expert")
    core, side, line = lax.rem(me, 2), lax.rem(me // 2, 2), me // 4
    tok_count, width = tokens.shape
    hid = hidden.shape[1]
    total_rows = 4 * depth * tok_count

    def device(z, x, c):
        return {"expert": (z * 2 + x) * 2 + c}

    def behind(step):
        pairs = (line, line + 1 - 2 * lax.rem(line, 2), lax.rem(line + 2, 4), 3 - line)
        return pairs[step]

    ahead = behind

    barrier = pltpu.get_barrier_semaphore()
    peers = [device(ahead(step), side, core) for step in range(1, depth)]
    side_peer = device(line, 1 - side, core)
    core_peer = device(line, side, 1 - core)
    for peer in peers + [side_peer, core_peer]:
        pl.semaphore_signal(barrier, inc=1, device_id=peer, device_id_type=MESH_ID)

    loads = [
        pltpu.make_async_copy(source, target, w_sem.at[i])
        for i, (source, target) in enumerate(
            ((gate_hbm.at[0], gate_w), (up_hbm.at[0], up_w), (down_hbm.at[0], down_w))
        )
    ]
    for load in loads:
        load.start()

    lane = lax.broadcasted_iota(jnp.int32, (tok_count, LANES), 1)
    place = lax.rem(lax.broadcasted_iota(jnp.int32, (LANES, tok_count), 0), experts)
    own_scale = keep[...].astype(jnp.float32) * weights[...]
    scale_own = jnp.zeros((LANES, tok_count), jnp.float32)
    for k in range(ids.shape[0]):
        scale_own = jnp.where(place == ids[k:k + 1, :], own_scale[k:k + 1, :], scale_own)
    scale_own = scale_own.T
    high = scale_own.astype(jnp.bfloat16).astype(jnp.float32)
    coded = jnp.where(lane < experts, high, scale_own - high)
    coded = jnp.where(lane < 2 * experts, coded, 0.0)
    rows[core, side, line, :, :width] = tokens[...]
    rows[core, side, line, :, width:] = coded.astype(jnp.bfloat16)
    grads[core, side, line] = cotangent[...]

    pl.semaphore_wait(barrier, depth + 1)

    sent = []

    def send(source, target, s_sem, r_sem, peer):
        copy = pltpu.make_async_remote_copy(
            src_ref=source, dst_ref=target, send_sem=s_sem, recv_sem=r_sem,
            device_id=peer, device_id_type=MESH_ID,
        )
        copy.start()
        sent.append(copy)

    def arrive(target, s_sem, r_sem, peer):
        pltpu.make_async_remote_copy(
            src_ref=target, dst_ref=target, send_sem=s_sem, recv_sem=r_sem,
            device_id=peer, device_id_type=MESH_ID,
        ).wait_recv()

    def share_step(buf, which, step):
        block = buf.at[core, side, behind(step)]
        send(block, block, side_s.at[which, step], side_r.at[which, step], side_peer)
        send(block, block, core_s.at[which, step], core_r.at[which, step], core_peer)

    def gather_start(buf, which):
        block = buf.at[core, side, line]
        share_step(buf, which, 0)
        for step in range(1, depth):
            send(block, block, line_s.at[which, step], line_r.at[which, step], peers[step - 1])

    def gather_line(buf, which):
        for step in range(1, depth):
            arrive(buf.at[core, side, behind(step)], line_s.at[which, step],
                   line_r.at[which, step], peers[step - 1])
            share_step(buf, which, step)

    def gather_side(buf, which):
        for step in range(depth):
            block = buf.at[core, 1 - side, behind(step)]
            arrive(block, side_s.at[which, step], side_r.at[which, step], side_peer)
            send(block, block, core_s.at[which, depth + step], core_r.at[which, depth + step],
                 core_peer)

    def gather_end(buf, which):
        for step in range(2 * depth):
            x = side if step < depth else 1 - side
            arrive(buf.at[1 - core, x, behind(step % depth)], core_s.at[which, step],
                   core_r.at[which, step], core_peer)

    gather_start(rows, 0)
    gather_line(rows, 0)
    gather_start(grads, 1)
    gather_side(rows, 0)
    gather_line(grads, 1)
    gather_end(rows, 0)
    loads[0].wait()
    loads[1].wait()

    tile = 256
    data = rows[:, :, :, :, :width].reshape(total_rows, width)
    lanes = lax.broadcasted_iota(jnp.int32, (total_rows, LANES), 1)
    coded_all = rows[:, :, :, :, width:].reshape(total_rows, LANES).astype(jnp.float32)
    mine = lax.rem(lanes, experts) == me
    scale = jnp.sum(jnp.where(mine, coded_all, 0.0), axis=1, keepdims=True)

    for t in range(hid // tile):
        cols = slice(t * tile, (t + 1) * tile)
        gate = jnp.dot(data, gate_w[:, cols], preferred_element_type=jnp.float32)
        up = jnp.dot(data, up_w[:, cols], preferred_element_type=jnp.float32)
        sig = jax.nn.sigmoid(gate)
        activated = gate * sig
        act[:, cols] = activated
        slope[:, cols] = up * sig * (1.0 + gate * (1.0 - sig))
        hidden[:, cols] = (activated * up).astype(jnp.bfloat16)

    def send_core(q):
        send(part[q].at[1 - core], from_core[q], a_s.at[q], a_r.at[q], core_peer)

    def send_side(q):
        arrive(from_core[q], a_s.at[q], a_r.at[q], core_peer)
        away = part[q][core, 1 - side].astype(jnp.float32)
        away = away + from_core[q][1 - side].astype(jnp.float32)
        to_side[q][...] = away.astype(jnp.bfloat16)
        send(to_side[q], from_side[q], b_s.at[q], b_r.at[q], side_peer)

    def send_line(q):
        arrive(from_side[q], b_s.at[q], b_r.at[q], side_peer)
        for step in range(1, depth):
            z = ahead(step)
            block = part[q][core, side, z].astype(jnp.float32)
            block = block + from_core[q][side, z].astype(jnp.float32)
            block = block + from_side[q][z].astype(jnp.float32)
            total[q][step] = block.astype(jnp.bfloat16)
            send(total[q].at[step], from_line[q].at[step], c_s.at[q, step], c_r.at[q, step],
                 peers[step - 1])

    def finish(q):
        block = part[q][core, side, line].astype(jnp.float32)
        block = block + from_core[q][side, line].astype(jnp.float32)
        block = block + from_side[q][line].astype(jnp.float32)
        for step in range(1, depth):
            arrive(from_line[q].at[step], c_s.at[q, step], c_r.at[q, step], peers[step - 1])
            block = block + from_line[q][step].astype(jnp.float32)
        return block

    half = count // 2
    cuts = []
    at = 0
    for q in range(half):
        cuts.append(slice(at, at + chunk[q]))
        at += chunk[q]
    shape = (2, 2, depth, tok_count)
    loads[2].wait()
    for q in range(half):
        out = jnp.dot(hidden[...], down_w[:, cuts[q]], preferred_element_type=jnp.float32)
        out = (scale * out).astype(jnp.bfloat16)
        part[q][...] = out.reshape(shape + (chunk[q],))
        send_core(q)
        if q >= 1:
            send_side(q - 1)
    gather_side(grads, 1)
    send_side(half - 1)
    gather_end(grads, 1)

    grad_data = grads[...].reshape(total_rows, width)
    dots = jnp.zeros((total_rows, 1), jnp.float32)
    contract = (((1,), (1,)), ((), ()))
    for t in range(hid // tile):
        cols = slice(t * tile, (t + 1) * tile)
        back = lax.dot_general(grad_data, down_w[cols, :], contract,
                               preferred_element_type=jnp.float32)
        dots = dots + jnp.sum(back * hidden[:, cols].astype(jnp.float32), axis=1, keepdims=True)
        back = back * scale
        d_gate[:, cols] = (back * slope[:, cols]).astype(jnp.bfloat16)
        d_up[:, cols] = (back * act[:, cols]).astype(jnp.bfloat16)
    dots_high = dots.astype(jnp.bfloat16).astype(jnp.float32)
    dots_coded = jnp.where(lanes < experts, dots_high, dots - dots_high)
    dots_coded = jnp.where(mine & (lanes < 2 * experts), dots_coded, 0.0).astype(jnp.bfloat16)

    for i in range(half):
        q = half + i
        wide = chunk[i]
        grad = lax.dot_general(d_gate[...], gate_w[cuts[i], :], contract,
                               preferred_element_type=jnp.float32)
        grad = grad + lax.dot_general(d_up[...], up_w[cuts[i], :], contract,
                                      preferred_element_type=jnp.float32)
        part[q][:, :, :, :, :wide] = grad.astype(jnp.bfloat16).reshape(shape + (wide,))
        if i == 0:
            part[q][:, :, :, :, wide:] = dots_coded.reshape(shape + (LANES,))
        send_core(q)
        if i >= 1:
            send_side(q - 1)
        send_line(i)
    send_side(count - 1)
    for q in range(half, count):
        send_line(q)
    for q in range(half):
        combined[:, cuts[q]] = finish(q).astype(jnp.bfloat16)
    for i in range(half):
        block = finish(half + i)
        grad_tokens[:, cuts[i]] = block[:, :chunk[i]].astype(jnp.bfloat16)
        if i == 0:
            tail = block[:, chunk[i]:]
            tail = jnp.where(lane < 2 * experts, tail, 0.0).T
            for k in range(ids.shape[0]):
                picked = jnp.where(place == ids[k:k + 1, :], tail, 0.0)
                picked = jnp.sum(picked, axis=0, keepdims=True)
                grad_weights[k:k + 1, :] = keep[k:k + 1, :].astype(jnp.float32) * picked
    for copy in sent:
        copy.wait_send()


def store_kernel(*refs):
    for i in range(3):
        refs[3 + i][...] = refs[i][...]


def local_fused(
    tokens, expert_ids, keep_flags, router_weights, grad_out, gate_weight, up_weight, down_weight
):
    depth = lax.axis_size("expert") // 4
    tok_count, width = tokens.shape
    hid = gate_weight.shape[2]
    total_rows = 4 * depth * tok_count
    pieces = 4
    each = width // pieces
    chunk = [each] * (2 * pieces)
    chunk[pieces] += LANES
    bf16, f32 = jnp.bfloat16, jnp.float32

    def blocks(*lead):
        return [pltpu.VMEM(lead + (tok_count, wide), bf16) for wide in chunk]

    scratch = [
        pltpu.VMEM((2, 2, depth, tok_count, width + LANES), bf16),
        pltpu.VMEM((2, 2, depth, tok_count, width), bf16),
        pltpu.VMEM(gate_weight.shape[1:], bf16),
        pltpu.VMEM(up_weight.shape[1:], bf16),
        pltpu.VMEM(down_weight.shape[1:], bf16),
        pltpu.VMEM((total_rows, hid), f32),
        pltpu.VMEM((total_rows, hid), f32),
        pltpu.VMEM((total_rows, hid), bf16),
        pltpu.VMEM((total_rows, hid), bf16),
        pltpu.VMEM((total_rows, hid), bf16),
        *blocks(2, 2, depth),
        *blocks(2, depth),
        *blocks(depth),
        *blocks(depth),
        *blocks(depth),
        *blocks(depth),
    ]
    sems = [(3,)] + [(2, depth)] * 4 + [(2, 2 * depth)] * 2
    sems += [(len(chunk),)] * 4 + [(len(chunk), depth)] * 2
    scratch += [pltpu.SemaphoreType.DMA(dims) for dims in sems]
    vmem = pl.BlockSpec(memory_space=pltpu.VMEM)
    far = pl.BlockSpec(memory_space=pl.ANY)
    results = pl.pallas_call(
        functools.partial(fused_kernel, depth, chunk),
        out_shape=(
            jax.ShapeDtypeStruct(tokens.shape, bf16),
            jax.ShapeDtypeStruct(tokens.shape, bf16),
            jax.ShapeDtypeStruct(router_weights.shape[::-1], f32),
        ),
        in_specs=[vmem] * 5 + [far] * 3,
        out_specs=(vmem, vmem, vmem),
        scratch_shapes=scratch,
        compiler_params=pltpu.CompilerParams(
            collective_id=0, has_side_effects=True, vmem_limit_bytes=56 * 1024 * 1024
        ),
        cost_estimate=pl.CostEstimate(
            flops=12 * total_rows * width * hid,
            bytes_accessed=6 * width * hid,
            transcendentals=total_rows * hid,
        ),
    )(tokens, expert_ids.T, keep_flags.T, router_weights.T, grad_out, gate_weight, up_weight,
      down_weight)
    combined, grad_tokens, grad_weights = pl.pallas_call(
        store_kernel,
        out_shape=tuple(jax.ShapeDtypeStruct(r.shape, r.dtype) for r in results),
        in_specs=[vmem] * 3,
        out_specs=(vmem,) * 3,
    )(*results)
    return combined, grad_tokens, grad_weights.T


def solution(mesh):
    sizes = mesh.shape
    dense = sizes["tensor"] == 1 and sizes["expert"] == 16
    local = local_fused if dense else local_exchange
    in_specs = (
        P(("groups", "expert"), None),
        P(("groups", "expert"), None),
        P(("groups", "expert"), None),
        P(("groups", "expert"), None),
        P(("groups", "expert"), "tensor"),
        P("expert", None, "tensor"),
        P("expert", None, "tensor"),
        P("expert", "tensor", None),
    )
    out_specs = (
        P(("groups", "expert"), "tensor"),
        P(("groups", "expert"), "tensor"),
        P(("groups", "expert"), None),
    )
    return jax.shard_map(local, mesh=mesh, in_specs=in_specs, out_specs=out_specs, check_vma=False)
```

```python
import functools

import jax
import jax.numpy as jnp
from jax import lax
from jax.experimental import pallas as pl
from jax.experimental.pallas import tpu as pltpu
from jax.sharding import PartitionSpec as P

LANES = 128
MESH_ID = pl.DeviceIdType.MESH


def route_tables(expert_ids, keep_flags, experts, capacity):
    tok_count, top_count = expert_ids.shape
    flat_ids = expert_ids.reshape(tok_count * top_count)
    onehot = (flat_ids[:, None] == jnp.arange(experts, dtype=jnp.int32)[None, :]).astype(jnp.int32)
    before = jnp.cumsum(onehot, axis=0) - onehot
    slot_rank = jnp.sum(before * onehot, axis=1)
    target = flat_ids * capacity + slot_rank
    picker = target[:, None] == jnp.arange(experts * capacity, dtype=jnp.int32)[None, :]
    kept = keep_flags.reshape(tok_count * top_count)[:, None] > 0
    sender = jnp.sum(
        (picker & kept).astype(jnp.bfloat16).reshape(tok_count, top_count, experts * capacity),
        axis=1,
    )
    return (picker.astype(jnp.bfloat16), sender)


def pack_rows(sender, source_cols, experts, capacity):
    packed = jnp.einsum("ts,td->sd", sender, source_cols, preferred_element_type=jnp.float32)
    return packed.astype(jnp.bfloat16).reshape(experts, capacity, source_cols.shape[1])


def local_exchange(
    tokens, expert_ids, keep_flags, router_weights, grad_out, gate_weight, up_weight, down_weight
):
    experts = lax.axis_size("expert")
    tok_count, top_count = expert_ids.shape
    capacity = min(tok_count, max(2, 2 * tok_count * top_count // experts))
    width = tokens.shape[1]
    width_half = grad_out.shape[1]
    gate_mat = gate_weight[0]
    up_mat = up_weight[0]
    down_mat = down_weight[0]
    picker, sender = route_tables(expert_ids, keep_flags, experts, capacity)
    keep_float = keep_flags.astype(jnp.float32)
    scale = keep_float * router_weights
    packed = pack_rows(sender, tokens, experts, capacity)
    received = lax.all_to_all(packed, "expert", split_axis=0, concat_axis=0, tiled=True)
    gate_pre = jnp.einsum("scd,dh->sch", received, gate_mat, preferred_element_type=jnp.float32)
    up_pre = jnp.einsum("scd,dh->sch", received, up_mat, preferred_element_type=jnp.float32)
    hidden = (jax.nn.silu(gate_pre) * up_pre).astype(jnp.bfloat16)
    partials = jnp.einsum("sch,hd->scd", hidden, down_mat, preferred_element_type=jnp.float32)
    partials, gate_pre, up_pre = (partials, gate_pre, up_pre)
    out_half = lax.psum_scatter(
        partials.astype(jnp.bfloat16), "tensor", scatter_dimension=2, tiled=True
    )
    returned = lax.all_to_all(out_half, "expert", split_axis=0, concat_axis=0, tiled=True).reshape(
        experts * capacity, width_half
    )
    out_assign = jnp.dot(picker, returned, preferred_element_type=jnp.float32).reshape(
        tok_count, top_count, width_half
    )
    combined = jnp.sum(scale[:, :, None] * out_assign, axis=1).astype(jnp.bfloat16)
    grad_float = grad_out.astype(jnp.float32)
    local_dots = keep_float * jnp.sum(grad_float[:, None, :] * out_assign, axis=2)
    grad_weights = lax.psum(local_dots, "tensor")
    grad_full = lax.all_gather(grad_out, "tensor", axis=1, tiled=True)
    grad_assign = (scale[:, :, None] * grad_full.astype(jnp.float32)[:, None, :]).astype(
        jnp.bfloat16
    )
    grad_assign = grad_assign.reshape(tok_count * top_count, width)
    grad_packed = jnp.einsum("as,ad->sd", picker, grad_assign, preferred_element_type=jnp.float32)
    grad_packed = grad_packed.astype(jnp.bfloat16).reshape(experts, capacity, width)
    grad_rows = lax.all_to_all(grad_packed, "expert", split_axis=0, concat_axis=0, tiled=True)
    grad_hidden = jnp.einsum("scd,hd->sch", grad_rows, down_mat, preferred_element_type=jnp.float32)
    sigmoid_gate = jax.nn.sigmoid(gate_pre)
    activated = gate_pre * sigmoid_gate
    grad_gate = (
        grad_hidden * up_pre * sigmoid_gate * (1.0 + gate_pre * (1.0 - sigmoid_gate))
    ).astype(jnp.bfloat16)
    grad_up = (grad_hidden * activated).astype(jnp.bfloat16)
    grad_part = jnp.einsum("sch,dh->scd", grad_gate, gate_mat, preferred_element_type=jnp.float32)
    grad_part = grad_part + jnp.einsum(
        "sch,dh->scd", grad_up, up_mat, preferred_element_type=jnp.float32
    )
    grad_half = lax.psum_scatter(
        grad_part.astype(jnp.bfloat16), "tensor", scatter_dimension=2, tiled=True
    )
    grad_back = lax.all_to_all(
        grad_half, "expert", split_axis=0, concat_axis=0, tiled=True
    ).reshape(experts * capacity, width_half)
    grad_picked = jnp.dot(picker, grad_back, preferred_element_type=jnp.float32).reshape(
        tok_count, top_count, width_half
    )
    grad_tokens = jnp.sum(grad_picked, axis=1).astype(jnp.bfloat16)
    return (combined, grad_tokens, grad_weights)


def fused_kernel(depth, chunk, tokens, ids, keep, weights, cotangent, gate_hbm, up_hbm, down_hbm,
                 combined, grad_tokens, grad_weights, rows, grads, gate_w, up_w, down_w, act, slope,
                 hidden, d_gate, d_up, *rest):
    count = len(chunk)
    part, from_core, to_side, from_side, total, from_line = (
        rest[i * count:(i + 1) * count] for i in range(6)
    )
    (w_sem, line_s, line_r, side_s, side_r, core_s, core_r,
     a_s, a_r, b_s, b_r, c_s, c_r) = rest[6 * count:]
    experts = lax.axis_size("expert")
    me = lax.axis_index("expert")
    core, side, line = lax.rem(me, 2), lax.rem(me // 2, 2), me // 4
    tok_count, width = tokens.shape
    hid = hidden.shape[1]
    total_rows = 4 * depth * tok_count

    def device(z, x, c):
        return {"expert": (z * 2 + x) * 2 + c}

    def behind(step):
        pairs = (line, line + 1 - 2 * lax.rem(line, 2), lax.rem(line + 2, 4), 3 - line)
        return pairs[step]

    ahead = behind

    barrier = pltpu.get_barrier_semaphore()
    peers = [device(ahead(step), side, core) for step in range(1, depth)]
    side_peer = device(line, 1 - side, core)
    core_peer = device(line, side, 1 - core)
    for peer in peers + [side_peer, core_peer]:
        pl.semaphore_signal(barrier, inc=1, device_id=peer, device_id_type=MESH_ID)

    loads = [
        pltpu.make_async_copy(source, target, w_sem.at[i])
        for i, (source, target) in enumerate(
            ((gate_hbm.at[0], gate_w), (up_hbm.at[0], up_w), (down_hbm.at[0], down_w))
        )
    ]
    for load in loads:
        load.start()

    lane = lax.broadcasted_iota(jnp.int32, (tok_count, LANES), 1)
    place = lax.rem(lax.broadcasted_iota(jnp.int32, (LANES, tok_count), 0), experts)
    own_scale = keep[...].astype(jnp.float32) * weights[...]
    scale_own = jnp.zeros((LANES, tok_count), jnp.float32)
    for k in range(ids.shape[0]):
        scale_own = jnp.where(place == ids[k:k + 1, :], own_scale[k:k + 1, :], scale_own)
    scale_own = scale_own.T
    high = scale_own.astype(jnp.bfloat16).astype(jnp.float32)
    coded = jnp.where(lane < experts, high, scale_own - high)
    coded = jnp.where(lane < 2 * experts, coded, 0.0)
    rows[core, side, line, :, :width] = tokens[...]
    rows[core, side, line, :, width:] = coded.astype(jnp.bfloat16)
    grads[core, side, line] = cotangent[...]

    pl.semaphore_wait(barrier, depth + 1)

    sent = []

    def send(source, target, s_sem, r_sem, peer):
        copy = pltpu.make_async_remote_copy(
            src_ref=source, dst_ref=target, send_sem=s_sem, recv_sem=r_sem,
            device_id=peer, device_id_type=MESH_ID,
        )
        copy.start()
        sent.append(copy)

    def arrive(target, s_sem, r_sem, peer):
        pltpu.make_async_remote_copy(
            src_ref=target, dst_ref=target, send_sem=s_sem, recv_sem=r_sem,
            device_id=peer, device_id_type=MESH_ID,
        ).wait_recv()

    def share_step(buf, which, step):
        block = buf.at[core, side, behind(step)]
        send(block, block, side_s.at[which, step], side_r.at[which, step], side_peer)
        send(block, block, core_s.at[which, step], core_r.at[which, step], core_peer)

    def gather_start(buf, which):
        block = buf.at[core, side, line]
        share_step(buf, which, 0)
        for step in range(1, depth):
            send(block, block, line_s.at[which, step], line_r.at[which, step], peers[step - 1])

    def gather_line(buf, which):
        for step in range(1, depth):
            arrive(buf.at[core, side, behind(step)], line_s.at[which, step],
                   line_r.at[which, step], peers[step - 1])
            share_step(buf, which, step)

    def gather_side(buf, which):
        for step in range(depth):
            block = buf.at[core, 1 - side, behind(step)]
            arrive(block, side_s.at[which, step], side_r.at[which, step], side_peer)
            send(block, block, core_s.at[which, depth + step], core_r.at[which, depth + step],
                 core_peer)

    def gather_end(buf, which):
        for step in range(2 * depth):
            x = side if step < depth else 1 - side
            arrive(buf.at[1 - core, x, behind(step % depth)], core_s.at[which, step],
                   core_r.at[which, step], core_peer)

    gather_start(rows, 0)
    gather_line(rows, 0)
    gather_start(grads, 1)
    gather_side(rows, 0)
    gather_line(grads, 1)
    gather_end(rows, 0)
    loads[0].wait()
    loads[1].wait()

    tile = 256
    data = rows[:, :, :, :, :width].reshape(total_rows, width)
    lanes = lax.broadcasted_iota(jnp.int32, (total_rows, LANES), 1)
    coded_all = rows[:, :, :, :, width:].reshape(total_rows, LANES).astype(jnp.float32)
    mine = lax.rem(lanes, experts) == me
    scale = jnp.sum(jnp.where(mine, coded_all, 0.0), axis=1, keepdims=True)

    for t in range(hid // tile):
        cols = slice(t * tile, (t + 1) * tile)
        gate = jnp.dot(data, gate_w[:, cols], preferred_element_type=jnp.float32)
        up = jnp.dot(data, up_w[:, cols], preferred_element_type=jnp.float32)
        sig = jax.nn.sigmoid(gate)
        activated = gate * sig
        act[:, cols] = activated
        slope[:, cols] = up * sig * (1.0 + gate * (1.0 - sig))
        hidden[:, cols] = (activated * up).astype(jnp.bfloat16)

    def send_core(q):
        send(part[q].at[1 - core], from_core[q], a_s.at[q], a_r.at[q], core_peer)

    def send_side(q):
        arrive(from_core[q], a_s.at[q], a_r.at[q], core_peer)
        away = part[q][core, 1 - side].astype(jnp.float32)
        away = away + from_core[q][1 - side].astype(jnp.float32)
        to_side[q][...] = away.astype(jnp.bfloat16)
        send(to_side[q], from_side[q], b_s.at[q], b_r.at[q], side_peer)

    def send_line(q):
        arrive(from_side[q], b_s.at[q], b_r.at[q], side_peer)
        for step in range(1, depth):
            z = ahead(step)
            block = part[q][core, side, z].astype(jnp.float32)
            block = block + from_core[q][side, z].astype(jnp.float32)
            block = block + from_side[q][z].astype(jnp.float32)
            total[q][step] = block.astype(jnp.bfloat16)
            send(total[q].at[step], from_line[q].at[step], c_s.at[q, step], c_r.at[q, step],
                 peers[step - 1])

    def finish(q):
        block = part[q][core, side, line].astype(jnp.float32)
        block = block + from_core[q][side, line].astype(jnp.float32)
        block = block + from_side[q][line].astype(jnp.float32)
        for step in range(1, depth):
            arrive(from_line[q].at[step], c_s.at[q, step], c_r.at[q, step], peers[step - 1])
            block = block + from_line[q][step].astype(jnp.float32)
        return block

    half = count // 2
    cuts = []
    at = 0
    for q in range(half):
        cuts.append(slice(at, at + chunk[q]))
        at += chunk[q]
    shape = (2, 2, depth, tok_count)
    loads[2].wait()
    for q in range(half):
        out = jnp.dot(hidden[...], down_w[:, cuts[q]], preferred_element_type=jnp.float32)
        out = (scale * out).astype(jnp.bfloat16)
        part[q][...] = out.reshape(shape + (chunk[q],))
        send_core(q)
    gather_side(grads, 1)
    for q in range(half):
        send_side(q)
    gather_end(grads, 1)

    grad_data = grads[...].reshape(total_rows, width)
    dots = jnp.zeros((total_rows, 1), jnp.float32)
    contract = (((1,), (1,)), ((), ()))
    for t in range(hid // tile):
        cols = slice(t * tile, (t + 1) * tile)
        back = lax.dot_general(grad_data, down_w[cols, :], contract,
                               preferred_element_type=jnp.float32)
        dots = dots + jnp.sum(back * hidden[:, cols].astype(jnp.float32), axis=1, keepdims=True)
        back = back * scale
        d_gate[:, cols] = (back * slope[:, cols]).astype(jnp.bfloat16)
        d_up[:, cols] = (back * act[:, cols]).astype(jnp.bfloat16)
    dots_high = dots.astype(jnp.bfloat16).astype(jnp.float32)
    dots_coded = jnp.where(lanes < experts, dots_high, dots - dots_high)
    dots_coded = jnp.where(mine & (lanes < 2 * experts), dots_coded, 0.0).astype(jnp.bfloat16)

    for i in range(half):
        q = half + i
        wide = chunk[i]
        grad = lax.dot_general(d_gate[...], gate_w[cuts[i], :], contract,
                               preferred_element_type=jnp.float32)
        grad = grad + lax.dot_general(d_up[...], up_w[cuts[i], :], contract,
                                      preferred_element_type=jnp.float32)
        part[q][:, :, :, :, :wide] = grad.astype(jnp.bfloat16).reshape(shape + (wide,))
        if i == 0:
            part[q][:, :, :, :, wide:] = dots_coded.reshape(shape + (LANES,))
        send_core(q)
        if i >= 1:
            send_side(q - 1)
        send_line(i)
    send_side(count - 1)
    for q in range(half, count):
        send_line(q)
    for q in range(half):
        combined[:, cuts[q]] = finish(q).astype(jnp.bfloat16)
    for i in range(half):
        block = finish(half + i)
        grad_tokens[:, cuts[i]] = block[:, :chunk[i]].astype(jnp.bfloat16)
        if i == 0:
            tail = block[:, chunk[i]:]
            tail = jnp.where(lane < 2 * experts, tail, 0.0).T
            for k in range(ids.shape[0]):
                picked = jnp.where(place == ids[k:k + 1, :], tail, 0.0)
                picked = jnp.sum(picked, axis=0, keepdims=True)
                grad_weights[k:k + 1, :] = keep[k:k + 1, :].astype(jnp.float32) * picked
    for copy in sent:
        copy.wait_send()


def store_kernel(*refs):
    for i in range(3):
        refs[3 + i][...] = refs[i][...]


def local_fused(
    tokens, expert_ids, keep_flags, router_weights, grad_out, gate_weight, up_weight, down_weight
):
    depth = lax.axis_size("expert") // 4
    tok_count, width = tokens.shape
    hid = gate_weight.shape[2]
    total_rows = 4 * depth * tok_count
    pieces = 4
    each = width // pieces
    chunk = [each] * (2 * pieces)
    chunk[pieces] += LANES
    bf16, f32 = jnp.bfloat16, jnp.float32

    def blocks(*lead):
        return [pltpu.VMEM(lead + (tok_count, wide), bf16) for wide in chunk]

    scratch = [
        pltpu.VMEM((2, 2, depth, tok_count, width + LANES), bf16),
        pltpu.VMEM((2, 2, depth, tok_count, width), bf16),
        pltpu.VMEM(gate_weight.shape[1:], bf16),
        pltpu.VMEM(up_weight.shape[1:], bf16),
        pltpu.VMEM(down_weight.shape[1:], bf16),
        pltpu.VMEM((total_rows, hid), f32),
        pltpu.VMEM((total_rows, hid), f32),
        pltpu.VMEM((total_rows, hid), bf16),
        pltpu.VMEM((total_rows, hid), bf16),
        pltpu.VMEM((total_rows, hid), bf16),
        *blocks(2, 2, depth),
        *blocks(2, depth),
        *blocks(depth),
        *blocks(depth),
        *blocks(depth),
        *blocks(depth),
    ]
    sems = [(3,)] + [(2, depth)] * 4 + [(2, 2 * depth)] * 2
    sems += [(len(chunk),)] * 4 + [(len(chunk), depth)] * 2
    scratch += [pltpu.SemaphoreType.DMA(dims) for dims in sems]
    vmem = pl.BlockSpec(memory_space=pltpu.VMEM)
    far = pl.BlockSpec(memory_space=pl.ANY)
    results = pl.pallas_call(
        functools.partial(fused_kernel, depth, chunk),
        out_shape=(
            jax.ShapeDtypeStruct(tokens.shape, bf16),
            jax.ShapeDtypeStruct(tokens.shape, bf16),
            jax.ShapeDtypeStruct(router_weights.shape[::-1], f32),
        ),
        in_specs=[vmem] * 5 + [far] * 3,
        out_specs=(vmem, vmem, vmem),
        scratch_shapes=scratch,
        compiler_params=pltpu.CompilerParams(
            collective_id=0, has_side_effects=True, vmem_limit_bytes=56 * 1024 * 1024
        ),
        cost_estimate=pl.CostEstimate(
            flops=12 * total_rows * width * hid,
            bytes_accessed=6 * width * hid,
            transcendentals=total_rows * hid,
        ),
    )(tokens, expert_ids.T, keep_flags.T, router_weights.T, grad_out, gate_weight, up_weight,
      down_weight)
    combined, grad_tokens, grad_weights = pl.pallas_call(
        store_kernel,
        out_shape=tuple(jax.ShapeDtypeStruct(r.shape, r.dtype) for r in results),
        in_specs=[vmem] * 3,
        out_specs=(vmem,) * 3,
    )(*results)
    return combined, grad_tokens, grad_weights.T


def solution(mesh):
    sizes = mesh.shape
    dense = sizes["tensor"] == 1 and sizes["expert"] == 16
    local = local_fused if dense else local_exchange
    in_specs = (
        P(("groups", "expert"), None),
        P(("groups", "expert"), None),
        P(("groups", "expert"), None),
        P(("groups", "expert"), None),
        P(("groups", "expert"), "tensor"),
        P("expert", None, "tensor"),
        P("expert", None, "tensor"),
        P("expert", "tensor", None),
    )
    out_specs = (
        P(("groups", "expert"), "tensor"),
        P(("groups", "expert"), "tensor"),
        P(("groups", "expert"), None),
    )
    return jax.shard_map(local, mesh=mesh, in_specs=in_specs, out_specs=out_specs, check_vma=False)
```
